32 devices in a mesh: grp: 2 (over y), row: 4 (over z), col: 2 (over x), ka: 2 (over core).
Axes of the slice: x: 2, y: 2, z: 4, core: 2. Of those that a mesh axis runs over, the one named last changes fastest.
Arguments:
- left_data: bfloat16 [4, 1024, 32, 256], P('grp', 'row', 'col', 'ka'), parts along dimension 0, may hold values from -6 to 6
- right_data: bfloat16 [4, 32, 256, 1024], P('grp', 'row', 'ka', 'col'), parts along dimension 0, may hold values from -0.125 to 0.125
- taper_table: float32 [8, 256], replicated, may hold values from 0.2 to 1
- pattern: int32 [64, 32], P('row'), may hold values from 0 to 1, as said below
- taper_index: int32 [64, 32], P('row'), may hold values from 0 to 7, as said below
Outputs:
- predicted: float32 [4, 1024, 1024], P('grp', 'row', ('col', 'ka')), parts along dimension 0
The draws below stay inside these ranges and needn't reach their ends.
There are 2 independent parts, one for each index of `grp`. The reference program is written for one: setup_inputs(seed, part) draws one part's arguments, and reference() takes and returns one part's arrays. A program takes and returns all parts, laid end to end along the dimension named above; an argument that names none is the same for every part. Nothing has to cross between parts.
Inputs may be any that keep to these rules, and one draw needn't show every extreme that they name: `pattern`: each receiver block's aperture is one contiguous run of inner blocks around the inner block nearest to it, cut at the ends of the range; its half width varies from block to block, up to 16. `taper_index`: inside an aperture the index grows with the distance from its centre; outside it is 7.
All inputs are finite; a program needn't handle non-finite values.
Results may differ from the reference program's by a relative error of at most 0.0029.
Values may be sent and summed in bfloat16 or wider, within the bound.
A program may use at most 128 MiB of HBM per device.

```python
import jax
import jax.numpy as jnp

KB = 32
KW = 256
NTAP = 8
K = 8192
R = 1024
RB = 64
S = 1024


def aperture_layout(key):
    width_key = jax.random.fold_in(key, 11)
    pick_key = jax.random.fold_in(key, 12)
    half_width = jax.random.randint(width_key, (RB,), 2, KB // 2 + 1)
    widest = jax.random.randint(pick_key, (), 0, RB)
    half_width = jnp.where(jnp.arange(RB, dtype=jnp.int32) == widest, KB // 2, half_width)
    centre = jnp.arange(RB, dtype=jnp.int32) * KB // RB
    distance = jnp.abs(jnp.arange(KB, dtype=jnp.int32)[None, :] - centre[:, None])
    inside = distance <= half_width[:, None]
    level = jnp.minimum(NTAP - 1, distance * NTAP // (half_width[:, None] + 1))
    return (inside.astype(jnp.int32), jnp.where(inside, level, NTAP - 1).astype(jnp.int32))


def draw_pattern(key, part):
    inside, level = aperture_layout(key)
    return inside


def draw_taper_index(key, part):
    inside, level = aperture_layout(key)
    return level


def steps_of(key, shape, cuts, smallest, largest):
    gain, own = 1.0, jax.random.fold_in(key, 6)
    for dim, shards_of in cuts:
        draws = jnp.exp(jax.random.uniform(jax.random.fold_in(own, dim), (shards_of,), jnp.float32, smallest / len(cuts), largest / len(cuts)))
        gain = gain * jnp.repeat(draws, shape[dim] // shards_of).reshape([-1 if axis == dim else 1 for axis in range(len(shape))])
    return gain


def centred(key, extent, scale, reach, cuts=(), kind=jnp.bfloat16):
    loudness = steps_of(key, extent, cuts, -0.22, 0.18) if cuts else 1.0
    values = jax.random.normal(key, extent, jnp.float32) * scale * loudness
    return jnp.minimum(jnp.maximum(values, -reach), reach).astype(kind)


def setup_inputs(seed: int = 0, part: int = 0) -> dict:
    streams_of = jax.random.split(jax.random.key(seed), 6)
    part_keys = jax.random.split(jax.random.fold_in(streams_of[5], part), 6)
    return {
        "left_data": centred(part_keys[0], (2, R, KB, KW), 1.0, 6.0, ((1, 4), (2, 2), (3, 2))),
        "right_data": centred(part_keys[1], (2, KB, KW, S), (K // 4) ** -0.5, 0.125, ((1, 4), (2, 2), (3, 2))),
        "taper_table": jnp.clip(jax.random.uniform(streams_of[2], (NTAP, KW), jnp.float32, 0.2, 1.0), 0.2, 1.0),
        "pattern": draw_pattern(jax.random.fold_in(streams_of[5], 71), part),
        "taper_index": draw_taper_index(jax.random.fold_in(streams_of[5], 71), part),
    }


def reference(left_data, right_data, taper_table, pattern, taper_index):
    weights = pattern.astype(jnp.float32)[:, :, None] * taper_table[taper_index]
    blocks = pattern.shape[0]
    rows = left_data.shape[1]
    shaped = left_data.astype(jnp.float32).reshape(2, blocks, rows // blocks, KB, KW) * weights[None, :, None]
    weighted = shaped.astype(jnp.bfloat16).reshape(2, rows, KB * KW)
    right = right_data.reshape(2, KB * KW, right_data.shape[3])
    real_part = jnp.dot(weighted[0], right[0], preferred_element_type=jnp.float32) - jnp.dot(weighted[1], right[1], preferred_element_type=jnp.float32)
    imag_part = jnp.dot(weighted[0], right[1], preferred_element_type=jnp.float32) + jnp.dot(weighted[1], right[0], preferred_element_type=jnp.float32)
    return jnp.stack([real_part, imag_part])
```

```python
import jax
import jax.numpy as jnp
from jax import lax
from jax.experimental import pallas as pl
from jax.experimental.pallas import tpu as pltpu
from jax.sharding import PartitionSpec as P


def blend(left_data, taper_table, pattern, taper_index):
    col_part = left_data.shape[2]
    width = left_data.shape[3]
    rows = left_data.shape[1]
    blocks = pattern.shape[0]
    col_start = lax.axis_index("col") * col_part
    ka_start = lax.axis_index("ka") * width
    used = lax.dynamic_slice_in_dim(pattern, col_start, col_part, 1).astype(jnp.float32)
    levels = lax.dynamic_slice_in_dim(taper_index, col_start, col_part, 1)
    table = lax.dynamic_slice_in_dim(taper_table, ka_start, width, 1)
    onehot = (
        levels[:, :, None] == jnp.arange(taper_table.shape[0], dtype=jnp.int32)[None, None, :]
    ).astype(jnp.float32)
    weights = used[:, :, None] * jnp.einsum(
        "bjt,tw->bjw", onehot, table, precision=lax.Precision.HIGHEST
    )
    shaped = (
        left_data.astype(jnp.float32).reshape(2, blocks, rows // blocks, col_part, width)
        * weights[None, :, None]
    )
    return shaped.reshape(left_data.shape).astype(jnp.bfloat16)


def make_step(panel):

    def contract(piece):
        terms = jnp.einsum("crjw,djws->cdrs", panel, piece, preferred_element_type=jnp.float32)
        return jnp.stack([terms[0, 0] - terms[1, 1], terms[0, 1] + terms[1, 0]])

    def step(carry, piece, start):
        return contract(piece)

    return step


def local(left_data, right_data, taper_table, pattern, taper_index):
    weighted = blend(left_data, taper_table, pattern, taper_index)
    rows = left_data.shape[1]
    halves = lax.all_gather(weighted, "ka", axis=3, tiled=True)
    panel = lax.all_gather(halves, "col", axis=2, tiled=True)
    columns = lax.all_to_all(right_data, "ka", split_axis=3, concat_axis=2, tiled=True)
    start_sum = jnp.zeros((2, rows, columns.shape[3]), jnp.float32)
    result = make_step(panel)(
        start_sum, lax.all_gather(columns, "row", axis=1, tiled=True), jnp.int32(0)
    )
    return result


MESH = pl.DeviceIdType.MESH
BAND = 32
OWN, PAIR, EDGE, NEAR = 0, 1, 2, 3


def kernel(w_ref, right_ref, out_ref, left, rights, part_out, part_in, send_out, recv_out,
           loc_sem, pair_sem, near_sem, edge_send, edge_recv, right_send, right_recv,
           part_send, part_recv, out_send, out_recv):
    row, col, ka = lax.axis_index("row"), lax.axis_index("col"), lax.axis_index("ka")
    side = row // 2
    half = row % 2
    computes = side == col
    toward = 1 - 2 * col
    inner = (row == 1) | (row == 2)
    depth = left.shape[3]
    groups = depth // 128
    rows = left.shape[2]
    wide = out_ref.shape[2]

    left[EDGE] = jnp.zeros(left.shape[1:], left.dtype)

    barrier = pltpu.get_barrier_semaphore()
    for step in range(1, 8):
        to = (row * 2 + col + step) % 8
        pl.semaphore_signal(barrier, inc=1, device_id={"row": to // 2, "col": to % 2}, device_id_type=MESH)
    pl.semaphore_signal(barrier, inc=1, device_id={"ka": 1 - ka}, device_id_type=MESH)
    pl.semaphore_wait(barrier, 8)

    def pair_copy():
        return pltpu.make_async_remote_copy(
            w_ref.at[1 - half], left.at[PAIR], pair_sem.at[0], pair_sem.at[1],
            device_id={"row": 2 * side + 1 - half}, device_id_type=MESH)

    def near_copy(src_half, to_row):
        return pltpu.make_async_remote_copy(
            w_ref.at[src_half], left.at[NEAR], near_sem.at[0], near_sem.at[1],
            device_id={"row": to_row}, device_id_type=MESH)

    def edge_copy(step, below, src_half, to_row):
        band = pl.ds(BAND * step, BAND)
        lanes = pl.ds(128 * step, depth - 128 * step) if below else pl.ds(0, 128 * (step + 1))
        return pltpu.make_async_remote_copy(
            w_ref.at[src_half, :, band, lanes], left.at[EDGE, :, band, lanes],
            edge_send.at[step], edge_recv.at[step],
            device_id={"row": to_row}, device_id_type=MESH)

    def right_copy(order):
        which = (1 - ka) if order == 0 else ka
        lanes = pl.ds(pl.multiple_of(which * wide, wide), wide)
        return pltpu.make_async_remote_copy(
            right_ref.at[:, :, lanes], rights.at[1, :, :, lanes],
            right_send.at[order], right_recv.at[order],
            device_id={"col": 1 - col}, device_id_type=MESH)

    def edges(act):
        to_row = row - 2 * toward
        src_half = to_row % 2
        for below in (True, False):
            @pl.when(col == (0 if below else 1))
            def _():
                for step in range(groups):
                    act(edge_copy(step, below, src_half, to_row))

    @pl.when(jnp.logical_not(computes))
    def _():
        right_copy(0).start()
        edges(lambda copy: copy.start())

        @pl.when(inner)
        def _():
            near_copy(1 - col, row - toward).start()

        right_copy(1).start()

    def own_left():
        return pltpu.make_async_copy(w_ref.at[half], left.at[OWN], loc_sem.at[0])

    def own_right():
        return pltpu.make_async_copy(right_ref, rights.at[0], loc_sem.at[1])

    def product(group, sel, which):
        lanes = pl.ds(pl.multiple_of(which * wide, wide), wide)
        dot = lambda a, b: jnp.dot(left[group, a], rights[sel, b, :, lanes], preferred_element_type=jnp.float32)
        return dot(0, 0) - dot(1, 1), dot(0, 1) + dot(1, 0)

    def part_copy(group, sel):
        return pltpu.make_async_remote_copy(
            part_out.at[group, sel], part_in.at[group, sel],
            part_send.at[group, sel], part_recv.at[group, sel],
            device_id={"ka": 1 - ka}, device_id_type=MESH)

    def row_of(group):
        pair = row + 1 - 2 * half
        return jnp.where(group == OWN, row, jnp.where(group == PAIR, pair, jnp.where(
            group == EDGE, row + 2 * toward, row + toward)))

    def out_copy(group, sel):
        to_col = col if sel == 0 else 1 - col
        return pltpu.make_async_remote_copy(
            send_out.at[group, sel], recv_out.at[row],
            out_send.at[group, sel], out_recv.at[row],
            device_id={"row": row_of(group), "col": to_col}, device_id_type=MESH)

    def give(group, sel):
        real, imag = product(group, sel, 1 - ka)
        part_out[group, sel, 0] = real
        part_out[group, sel, 1] = imag
        part_copy(group, sel).start()

    def keep(group, sel):
        real, imag = product(group, sel, ka)
        part_copy(group, sel).wait_recv()
        real = real + part_in[group, sel, 0]
        imag = imag + part_in[group, sel, 1]

        def send():
            send_out[group, sel, 0] = real.astype(jnp.bfloat16)
            send_out[group, sel, 1] = imag.astype(jnp.bfloat16)
            out_copy(group, sel).start()

        if sel == 1:
            send()
        else:
            @pl.when(group == OWN)
            def _():
                out_ref[0] = real
                out_ref[1] = imag

            pl.when(group != OWN)(send)

    @pl.when(computes)
    def _():
        pair_copy().start()
        own_left().start()
        own_right().start()
        own_left().wait()
        own_right().wait()

        @pl.loop(0, 2)
        def _(group):
            @pl.when(group == PAIR)
            def _():
                pair_copy().wait_recv()

            give(group, 0)
            keep(group, 0)

        right_copy(0).wait_recv()

        @pl.loop(0, 2)
        def _(group):
            give(group, 1)

        for below in (True, False):
            @pl.when(col == (0 if below else 1))
            def _():
                for step in range(groups):
                    edge_copy(step, below, 0, row).wait_recv()

        @pl.loop(2, jnp.where(inner, 4, 3))
        def _(group):
            @pl.when(group == NEAR)
            def _():
                near_copy(0, row).wait_recv()

            give(group, 0)
            keep(group, 0)
            give(group, 1)

        right_copy(1).wait_recv()

        @pl.loop(0, jnp.where(inner, 4, 3))
        def _(group):
            keep(group, 1)

    @pl.when(jnp.logical_not(computes))
    def _():
        out_ref[...] = jnp.zeros_like(out_ref)

    for source in range(4):
        far = jnp.abs(row - source)

        @pl.when((far <= 2) & jnp.logical_not(computes & (far == 0)))
        def _():
            pltpu.make_async_remote_copy(
                send_out.at[0, 0], recv_out.at[source], out_send.at[0, 0], out_recv.at[source],
                device_id={"ka": 1 - ka}, device_id_type=MESH).wait_recv()
            out_ref[...] += recv_out[source].astype(jnp.float32)

    @pl.when(computes)
    def _():
        pair_copy().wait_send()
        for group in range(4):
            def done(group=group):
                for sel in (0, 1):
                    part_copy(group, sel).wait_send()
                    if (group, sel) != (OWN, 0):
                        out_copy(group, sel).wait_send()

            if group == NEAR:
                pl.when(inner)(done)
            else:
                done()

    @pl.when(jnp.logical_not(computes))
    def _():
        edges(lambda copy: copy.wait_send())
        right_copy(0).wait_send()
        right_copy(1).wait_send()

        @pl.when(inner)
        def _():
            near_copy(1 - col, row - toward).wait_send()


def fused(left_data, right_data, taper_table, pattern, taper_index):
    weighted = blend(left_data, taper_table, pattern, taper_index)
    _, rows, blocks, width = left_data.shape
    depth = right_data.shape[1] * width
    sources = right_data.shape[3]
    panel = weighted.reshape(2, rows, blocks * width // depth, depth).transpose(2, 0, 1, 3)
    right = right_data.reshape(2, depth, sources)
    wide = sources // 2
    dma = pltpu.SemaphoreType.DMA
    vmem = pl.BlockSpec(memory_space=pltpu.VMEM)
    return pl.pallas_call(
        kernel,
        out_shape=jax.ShapeDtypeStruct((2, rows, wide), jnp.float32),
        in_specs=[vmem, vmem],
        out_specs=vmem,
        scratch_shapes=[
            pltpu.VMEM((4, 2, rows, depth), jnp.bfloat16),
            pltpu.VMEM((2, 2, depth, sources), jnp.bfloat16),
            pltpu.VMEM((4, 2, 2, rows, wide), jnp.float32),
            pltpu.VMEM((4, 2, 2, rows, wide), jnp.float32),
            pltpu.VMEM((4, 2, 2, rows, wide), jnp.bfloat16),
            pltpu.VMEM((4, 2, rows, wide), jnp.bfloat16),
            dma((2,)), dma((2,)), dma((2,)), dma((8,)), dma((8,)), dma((2,)), dma((2,)),
            dma((4, 2)), dma((4, 2)), dma((4, 2)), dma((4,)),
        ],
        compiler_params=pltpu.CompilerParams(
            collective_id=0, has_side_effects=True, vmem_limit_bytes=56 * 1024 * 1024
        ),
    )(panel, right)


def fits(mesh, left_data, right_data, pattern):
    n_row, n_col, n_ka = mesh.shape["row"], mesh.shape["col"], mesh.shape["ka"]
    blocks = left_data.shape[2]
    return (
        n_row == 4 and n_col == 2 and n_ka == 2 and blocks == 32 and pattern.shape[0] == 2 * blocks
        and left_data.shape[1] == 1024 and left_data.shape[3] == 256 and right_data.shape[3] == 1024
    )


def solution(mesh):
    placed = (
        P("grp", "row", "col", "ka"),
        P("grp", "row", "ka", "col"),
        P(),
        P("row", None),
        P("row", None),
    )

    def run(left_data, right_data, taper_table, pattern, taper_index):
        step = fused if fits(mesh, left_data, right_data, pattern) else local
        return jax.shard_map(
            step, mesh=mesh, in_specs=placed, out_specs=P("grp", "row", ("col", "ka")), check_vma=False
        )(left_data, right_data, taper_table, pattern, taper_index)

    return run
```

```python
import jax
import jax.numpy as jnp
from jax import lax
from jax.experimental import pallas as pl
from jax.experimental.pallas import tpu as pltpu
from jax.sharding import PartitionSpec as P


def blend(left_data, taper_table, pattern, taper_index):
    col_part = left_data.shape[2]
    width = left_data.shape[3]
    rows = left_data.shape[1]
    blocks = pattern.shape[0]
    col_start = lax.axis_index("col") * col_part
    ka_start = lax.axis_index("ka") * width
    used = lax.dynamic_slice_in_dim(pattern, col_start, col_part, 1).astype(jnp.float32)
    levels = lax.dynamic_slice_in_dim(taper_index, col_start, col_part, 1)
    table = lax.dynamic_slice_in_dim(taper_table, ka_start, width, 1)
    onehot = (
        levels[:, :, None] == jnp.arange(taper_table.shape[0], dtype=jnp.int32)[None, None, :]
    ).astype(jnp.float32)
    weights = used[:, :, None] * jnp.einsum(
        "bjt,tw->bjw", onehot, table, precision=lax.Precision.HIGHEST
    )
    shaped = (
        left_data.astype(jnp.float32).reshape(2, blocks, rows // blocks, col_part, width)
        * weights[None, :, None]
    )
    return shaped.reshape(left_data.shape).astype(jnp.bfloat16)


def make_step(panel):

    def contract(piece):
        terms = jnp.einsum("crjw,djws->cdrs", panel, piece, preferred_element_type=jnp.float32)
        return jnp.stack([terms[0, 0] - terms[1, 1], terms[0, 1] + terms[1, 0]])

    def step(carry, piece, start):
        return contract(piece)

    return step


def local(left_data, right_data, taper_table, pattern, taper_index):
    weighted = blend(left_data, taper_table, pattern, taper_index)
    rows = left_data.shape[1]
    halves = lax.all_gather(weighted, "ka", axis=3, tiled=True)
    panel = lax.all_gather(halves, "col", axis=2, tiled=True)
    columns = lax.all_to_all(right_data, "ka", split_axis=3, concat_axis=2, tiled=True)
    start_sum = jnp.zeros((2, rows, columns.shape[3]), jnp.float32)
    result = make_step(panel)(
        start_sum, lax.all_gather(columns, "row", axis=1, tiled=True), jnp.int32(0)
    )
    return result


MESH = pl.DeviceIdType.MESH
BAND = 32
THIN = 128
OWN, PAIR, EDGE, NEAR = 0, 1, 2, 3


def weigh(raw, table_ref, pattern_ref, index_ref, turned, weights, loose, panel, col, ka, ready):
    blocks, points = raw.shape[2], raw.shape[3]
    depth = panel.shape[3]
    turned[...] = jnp.zeros_like(turned)
    levels, many = pattern_ref.shape
    turned[0, 0:levels, 0:many] = pattern_ref[...].astype(jnp.float32)
    turned[1, 0:levels, 0:many] = index_ref[...].astype(jnp.float32)
    used = turned[0].T
    level = turned[1].T
    turned[0] = used
    turned[1] = level
    mine = pl.ds(pl.multiple_of(col * blocks, blocks), blocks)
    table = table_ref[:, pl.ds(pl.multiple_of(ka * points, points), points)]
    for block in range(levels):
        column = turned[1, mine, block:block + 1]
        total = jnp.zeros((blocks, points), jnp.float32)
        for tap in range(table.shape[0]):
            total = jnp.where(column == tap, table[tap:tap + 1, :], total)
        weights[block] = total * turned[0, mine, block:block + 1]
    tall = raw.shape[1] // levels
    per = depth // points
    for block in range(levels):
        for part in range(2):
            slot = (2 * block + part) % loose.shape[0]
            rows = slice(block * tall, (block + 1) * tall)
            values = raw[part, rows].astype(jnp.float32) * weights[block][None]
            loose[slot] = values.reshape(tall * blocks, points)
            for j in range(blocks):
                lane = (j % per) * points
                panel[j // per, part, rows, lane:lane + points] = loose[
                    slot, pl.ds(j, tall, stride=blocks), :].astype(jnp.bfloat16)
        if (block + 1) * tall % BAND == 0:
            ready((block + 1) * tall // BAND - 1)


def kernel(left_ref, right_ref, table_ref, pattern_ref, index_ref, out_ref,
           raw, turned, weights, loose, panel, left, rights, part_out, part_in, send_out, recv_out,
           loc_sem, pair_sem, near_sem, edge_send, edge_recv, right_send, right_recv,
           part_send, part_recv, out_send, out_recv):
    row, col, ka = lax.axis_index("row"), lax.axis_index("col"), lax.axis_index("ka")
    side = row // 2
    half = row % 2
    computes = side == col
    idle = jnp.logical_not(computes)
    toward = 1 - 2 * col
    inner = (row == 1) | (row == 2)
    depth = left.shape[3]
    groups = depth // 128
    wide = out_ref.shape[2]

    own_raw = pltpu.make_async_copy(left_ref, raw, loc_sem.at[0])
    own_raw.start()
    left[EDGE] = jnp.zeros(left.shape[1:], left.dtype)

    barrier = pltpu.get_barrier_semaphore()
    for step in range(1, 8):
        to = (row * 2 + col + step) % 8
        pl.semaphore_signal(barrier, inc=1, device_id={"row": to // 2, "col": to % 2}, device_id_type=MESH)
    pl.semaphore_signal(barrier, inc=1, device_id={"ka": 1 - ka}, device_id_type=MESH)
    pl.semaphore_wait(barrier, 8)

    def pair_copy():
        return pltpu.make_async_remote_copy(
            panel.at[1 - half], left.at[PAIR], pair_sem.at[0], pair_sem.at[1],
            device_id={"row": 2 * side + 1 - half}, device_id_type=MESH)

    def near_copy(src_half, to_row):
        return pltpu.make_async_remote_copy(
            panel.at[src_half], left.at[NEAR], near_sem.at[0], near_sem.at[1],
            device_id={"row": to_row}, device_id_type=MESH)

    def edge_copy(step, below, src_half, to_row):
        band = pl.ds(BAND * step, BAND)
        lanes = pl.ds(128 * step, depth - 128 * step) if below else pl.ds(0, 128 * (step + 1))
        return pltpu.make_async_remote_copy(
            panel.at[src_half, :, band, lanes], left.at[EDGE, :, band, lanes],
            edge_send.at[step], edge_recv.at[step],
            device_id={"row": to_row}, device_id_type=MESH)

    def edge(act, step):
        to_row = row - 2 * toward
        for below in (True, False):
            @pl.when(idle & (col == (0 if below else 1)))
            def _():
                act(edge_copy(step, below, to_row % 2, to_row))

    def right_copy(n):
        lanes = pl.ds(THIN * n, THIN)
        return pltpu.make_async_remote_copy(
            right_ref.at[:, :, lanes], rights.at[1, :, :, lanes],
            right_send.at[n], right_recv.at[n],
            device_id={"col": 1 - col}, device_id_type=MESH)

    def own_left():
        return pltpu.make_async_copy(panel.at[half], left.at[OWN], loc_sem.at[0])

    def own_right():
        return pltpu.make_async_copy(right_ref, rights.at[0], loc_sem.at[1])

    @pl.when(idle)
    def _():
        right_copy(0).start()
        right_copy(1).start()

    pl.when(computes)(lambda: own_right().start())

    own_raw.wait()
    weigh(raw, table_ref, pattern_ref, index_ref, turned, weights, loose, panel, col, ka,
          lambda step: edge(lambda copy: copy.start(), step))

    def part_copy(group, sel, start, size):
        here = pl.ds(start % wide, size)
        return pltpu.make_async_remote_copy(
            part_out.at[group, sel, :, :, pl.ds(start, size)], part_in.at[group, sel, :, :, here],
            part_send.at[group, sel, start // size % 2 if sel else 0],
            part_recv.at[group, sel, start // size % 2 if sel else 0],
            device_id={"ka": 1 - ka}, device_id_type=MESH)

    def row_of(group):
        pair = row + 1 - 2 * half
        return jnp.where(group == OWN, row, jnp.where(group == PAIR, pair, jnp.where(
            group == EDGE, row + 2 * toward, row + toward)))

    def out_copy(group, sel, start, size):
        here = pl.ds(start % wide, size)
        to_col = col if sel == 0 else 1 - col
        which = start // size % 2 if sel else 0
        return pltpu.make_async_remote_copy(
            send_out.at[group, sel, :, :, here], recv_out.at[row, :, :, here],
            out_send.at[group, sel, which], out_recv.at[row, which],
            device_id={"row": row_of(group), "col": to_col}, device_id_type=MESH)

    def unit(group, sel, start, size):
        lanes = slice(start, start + size)
        here = slice(start % wide, start % wide + size)
        dot = lambda a, b: jnp.dot(left[group, a], rights[sel, b, :, lanes], preferred_element_type=jnp.float32)
        part_out[group, sel, 0, :, lanes] = dot(0, 0) - dot(1, 1)
        part_out[group, sel, 1, :, lanes] = dot(0, 1) + dot(1, 0)

        @pl.when(ka != start // wide)
        def _():
            part_copy(group, sel, start, size).start()

        @pl.when(ka == start // wide)
        def _():
            part_copy(group, sel, start, size).wait_recv()

            def total():
                return part_out[group, sel, :, :, lanes] + part_in[group, sel, :, :, here]

            def send():
                send_out[group, sel, :, :, here] = total().astype(jnp.bfloat16)
                out_copy(group, sel, start, size).start()

            if sel == 1:
                send()
            else:
                @pl.when(group == OWN)
                def _():
                    out_ref[...] = total()

                pl.when(group != OWN)(send)

    def local_units(group):
        for start in range(0, 2 * wide, wide):
            unit(group, 0, start, wide)

    held = jnp.where(inner, 4, 3)

    @pl.when(computes)
    def _():
        pair_copy().start()
        own_left().start()
        own_right().wait()
        own_left().wait()

        local_units(OWN)
        right_copy(0).wait_recv()
        unit(OWN, 1, 0, THIN)

        pair_copy().wait_recv()
        local_units(PAIR)
        unit(PAIR, 1, 0, THIN)
        right_copy(1).wait_recv()

        @pl.loop(0, 2)
        def _(group):
            unit(group, 1, THIN, THIN)

        for below in (True, False):
            @pl.when(col == (0 if below else 1))
            def _():
                for step in range(groups):
                    edge_copy(step, below, 0, row).wait_recv()

        local_units(EDGE)
        unit(EDGE, 1, 0, THIN)
        unit(EDGE, 1, THIN, THIN)
        right_copy(2).wait_recv()

        @pl.loop(0, 3)
        def _(group):
            unit(group, 1, 2 * THIN, THIN)

        right_copy(3).wait_recv()

        @pl.loop(0, 3)
        def _(group):
            unit(group, 1, 3 * THIN, THIN)

        @pl.when(inner)
        def _():
            near_copy(0, row).wait_recv()
            for n in range(4):
                unit(NEAR, 1, n * THIN, THIN)
            local_units(NEAR)

    @pl.when(idle)
    def _():
        right_copy(0).wait_send()
        right_copy(2).start()
        for step in range(groups):
            edge(lambda copy: copy.wait_send(), step)

        @pl.when(inner)
        def _():
            near_copy(1 - col, row - toward).start()

        right_copy(1).wait_send()
        right_copy(3).start()
        out_ref[...] = jnp.zeros_like(out_ref)

    for source in (0, 3, 1, 2):
        far = jnp.abs(row - source)
        crosses = col != source // 2

        @pl.when((far <= 2) & jnp.logical_not(computes & (far == 0)))
        def _():
            def arrive(which, lanes):
                pltpu.make_async_remote_copy(
                    send_out.at[0, 0, :, :, lanes], recv_out.at[source, :, :, lanes],
                    out_send.at[0, 0, 0], out_recv.at[source, which],
                    device_id={"ka": 1 - ka}, device_id_type=MESH).wait_recv()

            @pl.when(crosses)
            def _():
                arrive(0, pl.ds(0, THIN))
                arrive(1, pl.ds(THIN, THIN))

            @pl.when(jnp.logical_not(crosses))
            def _():
                arrive(0, pl.ds(0, wide))

            out_ref[...] += recv_out[source].astype(jnp.float32)

    @pl.when(computes)
    def _():
        pair_copy().wait_send()
        for group in range(4):
            def done(group=group):
                for sel, size in ((0, wide), (1, THIN)):
                    for start in range(0, 2 * wide, size):
                        @pl.when(ka != start // wide)
                        def _():
                            part_copy(group, sel, start, size).wait_send()

                        if (group, sel) != (OWN, 0):
                            @pl.when(ka == start // wide)
                            def _():
                                out_copy(group, sel, start, size).wait_send()

            if group == NEAR:
                pl.when(inner)(done)
            else:
                done()

    @pl.when(idle)
    def _():
        right_copy(2).wait_send()
        right_copy(3).wait_send()

        @pl.when(inner)
        def _():
            near_copy(1 - col, row - toward).wait_send()


def fused(left_data, right_data, taper_table, pattern, taper_index):
    _, rows, blocks, width = left_data.shape
    depth = right_data.shape[1] * width
    sources = right_data.shape[3]
    right = right_data.reshape(2, depth, sources)
    wide = sources // 2
    dma = pltpu.SemaphoreType.DMA
    vmem, whole = pl.BlockSpec(memory_space=pltpu.VMEM), pl.BlockSpec(memory_space=pl.ANY)
    return pl.pallas_call(
        kernel,
        out_shape=jax.ShapeDtypeStruct((2, rows, wide), jnp.float32),
        in_specs=[whole, whole, vmem, vmem, vmem],
        out_specs=vmem,
        scratch_shapes=[
            pltpu.VMEM(left_data.shape, jnp.bfloat16),
            pltpu.VMEM((2, 128, 128), jnp.float32),
            pltpu.VMEM((pattern.shape[0], blocks, width), jnp.float32),
            pltpu.VMEM((4, rows // pattern.shape[0] * blocks, width), jnp.float32),
            pltpu.VMEM((2, 2, rows, depth), jnp.bfloat16),
            pltpu.VMEM((4, 2, rows, depth), jnp.bfloat16),
            pltpu.VMEM((2, 2, depth, sources), jnp.bfloat16),
            pltpu.VMEM((4, 2, 2, rows, sources), jnp.float32),
            pltpu.VMEM((4, 2, 2, rows, wide), jnp.float32),
            pltpu.VMEM((4, 2, 2, rows, wide), jnp.bfloat16),
            pltpu.VMEM((4, 2, rows, wide), jnp.bfloat16),
            dma((2,)), dma((2,)), dma((2,)), dma((8,)), dma((8,)), dma((4,)), dma((4,)),
            dma((4, 2, 2)), dma((4, 2, 2)), dma((4, 2, 2)), dma((4, 2)),
        ],
        compiler_params=pltpu.CompilerParams(
            collective_id=0, has_side_effects=True, vmem_limit_bytes=60 * 1024 * 1024
        ),
    )(left_data, right, taper_table, pattern, taper_index)


def fits(mesh, left_data, right_data, pattern):
    n_row, n_col, n_ka = mesh.shape["row"], mesh.shape["col"], mesh.shape["ka"]
    blocks = left_data.shape[2]
    return (
        n_row == 4 and n_col == 2 and n_ka == 2 and blocks == 32 and pattern.shape[0] == 2 * blocks
        and left_data.shape[1] == 1024 and left_data.shape[3] == 256 and right_data.shape[3] == 1024
    )


def solution(mesh):
    placed = (
        P("grp", "row", "col", "ka"),
        P("grp", "row", "ka", "col"),
        P(),
        P("row", None),
        P("row", None),
    )

    def run(left_data, right_data, taper_table, pattern, taper_index):
        step = fused if fits(mesh, left_data, right_data, pattern) else local
        return jax.shard_map(
            step, mesh=mesh, in_specs=placed, out_specs=P("grp", "row", ("col", "ka")), check_vma=False
        )(left_data, right_data, taper_table, pattern, taper_index)

    return run
```

```python
import jax
import jax.numpy as jnp
from jax import lax
from jax.experimental import pallas as pl
from jax.experimental.pallas import tpu as pltpu
from jax.sharding import PartitionSpec as P


def blend(left_data, taper_table, pattern, taper_index):
    col_part = left_data.shape[2]
    width = left_data.shape[3]
    rows = left_data.shape[1]
    blocks = pattern.shape[0]
    col_start = lax.axis_index("col") * col_part
    ka_start = lax.axis_index("ka") * width
    used = lax.dynamic_slice_in_dim(pattern, col_start, col_part, 1).astype(jnp.float32)
    levels = lax.dynamic_slice_in_dim(taper_index, col_start, col_part, 1)
    table = lax.dynamic_slice_in_dim(taper_table, ka_start, width, 1)
    onehot = (
        levels[:, :, None] == jnp.arange(taper_table.shape[0], dtype=jnp.int32)[None, None, :]
    ).astype(jnp.float32)
    weights = used[:, :, None] * jnp.einsum(
        "bjt,tw->bjw", onehot, table, precision=lax.Precision.HIGHEST
    )
    shaped = (
        left_data.astype(jnp.float32).reshape(2, blocks, rows // blocks, col_part, width)
        * weights[None, :, None]
    )
    return shaped.reshape(left_data.shape).astype(jnp.bfloat16)


def make_step(panel):

    def contract(piece):
        terms = jnp.einsum("crjw,djws->cdrs", panel, piece, preferred_element_type=jnp.float32)
        return jnp.stack([terms[0, 0] - terms[1, 1], terms[0, 1] + terms[1, 0]])

    def step(carry, piece, start):
        return contract(piece)

    return step


def local(left_data, right_data, taper_table, pattern, taper_index):
    weighted = blend(left_data, taper_table, pattern, taper_index)
    rows = left_data.shape[1]
    halves = lax.all_gather(weighted, "ka", axis=3, tiled=True)
    panel = lax.all_gather(halves, "col", axis=2, tiled=True)
    columns = lax.all_to_all(right_data, "ka", split_axis=3, concat_axis=2, tiled=True)
    start_sum = jnp.zeros((2, rows, columns.shape[3]), jnp.float32)
    result = make_step(panel)(
        start_sum, lax.all_gather(columns, "row", axis=1, tiled=True), jnp.int32(0)
    )
    return result


MESH = pl.DeviceIdType.MESH
BAND = 32
THIN = 128
OWN, PAIR, EDGE, NEAR = 0, 1, 2, 3


def weigh(raw, table_ref, pattern_ref, index_ref, turned, weights, loose, panel, col, ka, ready):
    blocks, points = raw.shape[2], raw.shape[3]
    depth = panel.shape[3]
    turned[...] = jnp.zeros_like(turned)
    levels, many = pattern_ref.shape
    turned[0, 0:levels, 0:many] = pattern_ref[...].astype(jnp.float32)
    turned[1, 0:levels, 0:many] = index_ref[...].astype(jnp.float32)
    used = turned[0].T
    level = turned[1].T
    turned[0] = used
    turned[1] = level
    mine = pl.ds(pl.multiple_of(col * blocks, blocks), blocks)
    table = table_ref[:, pl.ds(pl.multiple_of(ka * points, points), points)]
    for block in range(levels):
        column = turned[1, mine, block:block + 1]
        total = jnp.zeros((blocks, points), jnp.float32)
        for tap in range(table.shape[0]):
            total = jnp.where(column == tap, table[tap:tap + 1, :], total)
        weights[block] = total * turned[0, mine, block:block + 1]
    tall = raw.shape[1] // levels
    per = depth // points
    for block in range(levels):
        for part in range(2):
            slot = (2 * block + part) % loose.shape[0]
            rows = slice(block * tall, (block + 1) * tall)
            values = raw[part, rows].astype(jnp.float32) * weights[block][None]
            loose[slot] = values.reshape(tall * blocks, points)
            for j in range(blocks):
                lane = (j % per) * points
                panel[j // per, part, rows, lane:lane + points] = loose[
                    slot, pl.ds(j, tall, stride=blocks), :].astype(jnp.bfloat16)
        if (block + 1) * tall % BAND == 0:
            ready((block + 1) * tall // BAND - 1)


def kernel(left_ref, right_ref, table_ref, pattern_ref, index_ref, out_ref,
           raw, turned, weights, loose, panel, left, rights, part_out, part_in, send_out, recv_out,
           relay_in, relay_out, loc_sem, pair_sem, near_sem, edge_send, edge_recv, right_send, right_recv,
           part_send, part_recv, out_send, out_recv, relay_recv, relay_send):
    row, col, ka = lax.axis_index("row"), lax.axis_index("col"), lax.axis_index("ka")
    side = row // 2
    half = row % 2
    computes = side == col
    idle = jnp.logical_not(computes)
    toward = 1 - 2 * col
    inner = (row == 1) | (row == 2)
    depth = left.shape[3]
    groups = depth // 128
    wide = out_ref.shape[2]

    own_raw = pltpu.make_async_copy(left_ref, raw, loc_sem.at[0])
    own_raw.start()
    left[EDGE] = jnp.zeros(left.shape[1:], left.dtype)

    barrier = pltpu.get_barrier_semaphore()
    for step in range(1, 8):
        to = (row * 2 + col + step) % 8
        pl.semaphore_signal(barrier, inc=1, device_id={"row": to // 2, "col": to % 2}, device_id_type=MESH)
    pl.semaphore_signal(barrier, inc=1, device_id={"ka": 1 - ka}, device_id_type=MESH)
    pl.semaphore_wait(barrier, 8)

    def pair_copy():
        return pltpu.make_async_remote_copy(
            panel.at[1 - half], left.at[PAIR], pair_sem.at[0], pair_sem.at[1],
            device_id={"row": 2 * side + 1 - half}, device_id_type=MESH)

    def near_copy(src_half, to_row):
        return pltpu.make_async_remote_copy(
            panel.at[src_half], left.at[NEAR], near_sem.at[0], near_sem.at[1],
            device_id={"row": to_row}, device_id_type=MESH)

    def edge_copy(step, below, src_half, to_row):
        band = pl.ds(BAND * step, BAND)
        lanes = pl.ds(128 * step, depth - 128 * step) if below else pl.ds(0, 128 * (step + 1))
        return pltpu.make_async_remote_copy(
            panel.at[src_half, :, band, lanes], left.at[EDGE, :, band, lanes],
            edge_send.at[step], edge_recv.at[step],
            device_id={"row": to_row}, device_id_type=MESH)

    def edge(act, step):
        to_row = row - 2 * toward
        for below in (True, False):
            @pl.when(idle & (col == (0 if below else 1)))
            def _():
                act(edge_copy(step, below, to_row % 2, to_row))

    def right_copy(n):
        lanes = pl.ds(THIN * n, THIN)
        return pltpu.make_async_remote_copy(
            right_ref.at[:, :, lanes], rights.at[1, :, :, lanes],
            right_send.at[n], right_recv.at[n],
            device_id={"col": 1 - col}, device_id_type=MESH)

    def own_left():
        return pltpu.make_async_copy(panel.at[half], left.at[OWN], loc_sem.at[0])

    def own_right():
        return pltpu.make_async_copy(right_ref, rights.at[0], loc_sem.at[1])

    @pl.when(idle)
    def _():
        right_copy(0).start()
        right_copy(1).start()

    pl.when(computes)(lambda: own_right().start())

    own_raw.wait()
    weigh(raw, table_ref, pattern_ref, index_ref, turned, weights, loose, panel, col, ka,
          lambda step: edge(lambda copy: copy.start(), step))

    def part_copy(group, sel, start, size):
        here = pl.ds(start % wide, size)
        return pltpu.make_async_remote_copy(
            part_out.at[group, sel, :, :, pl.ds(start, size)], part_in.at[group, sel, :, :, here],
            part_send.at[group, sel, start // size % 2 if sel else 0],
            part_recv.at[group, sel, start // size % 2 if sel else 0],
            device_id={"ka": 1 - ka}, device_id_type=MESH)

    def row_of(group):
        pair = row + 1 - 2 * half
        return jnp.where(group == OWN, row, jnp.where(group == PAIR, pair, jnp.where(
            group == EDGE, row + 2 * toward, row + toward)))

    def out_copy(group, sel, start, size):
        here = pl.ds(start % wide, size)
        to_col = col if sel == 0 else 1 - col
        which = start // size % 2 if sel else 0
        return pltpu.make_async_remote_copy(
            send_out.at[group, sel, :, :, here], recv_out.at[row, :, :, here],
            out_send.at[group, sel, which], out_recv.at[row, which],
            device_id={"row": row_of(group), "col": to_col}, device_id_type=MESH)

    def relay_copy(group, start, size):
        here = pl.ds(start % wide, size)
        which = start // size % 2
        return pltpu.make_async_remote_copy(
            send_out.at[group, 1, :, :, here], relay_in.at[half, :, :, here],
            out_send.at[group, 1, which], relay_recv.at[half, which],
            device_id={"row": row_of(group)}, device_id_type=MESH)

    def forward_copy(which):
        here = pl.ds(which * THIN, THIN)
        return pltpu.make_async_remote_copy(
            relay_out.at[:, :, here], recv_out.at[2 * col, :, :, here],
            relay_send.at[which], out_recv.at[2 * col, which],
            device_id={"col": 1 - col}, device_id_type=MESH)

    def multiply(group, sel, start, size):
        lanes = slice(start, start + size)
        dot = lambda a, b: jnp.dot(left[group, a], rights[sel, b, :, lanes], preferred_element_type=jnp.float32)
        part_out[group, sel, 0, :, lanes] = dot(0, 0) - dot(1, 1)
        part_out[group, sel, 1, :, lanes] = dot(0, 1) + dot(1, 0)

        @pl.when(ka != start // wide)
        def _():
            part_copy(group, sel, start, size).start()

    def keep(group, sel, start, size):
        lanes = slice(start, start + size)
        here = slice(start % wide, start % wide + size)

        @pl.when(ka == start // wide)
        def _():
            part_copy(group, sel, start, size).wait_recv()

            def total():
                return part_out[group, sel, :, :, lanes] + part_in[group, sel, :, :, here]

            def send():
                send_out[group, sel, :, :, here] = total().astype(jnp.bfloat16)
                out_copy(group, sel, start, size).start()

            if sel == 1:
                send_out[group, sel, :, :, here] = total().astype(jnp.bfloat16)

                @pl.when(group < EDGE)
                def _():
                    out_copy(group, sel, start, size).start()

                @pl.when(group >= EDGE)
                def _():
                    relay_copy(group, start, size).start()
            else:
                @pl.when(group == OWN)
                def _():
                    out_ref[...] = total()

                pl.when(group != OWN)(send)

    def local(act, group):
        for start in range(0, 2 * wide, wide):
            act(group, 0, start, wide)

    @pl.when(computes)
    def _():
        pair_copy().start()
        own_left().start()
        own_right().wait()
        own_left().wait()

        local(multiply, OWN)
        right_copy(0).wait_recv()
        multiply(OWN, 1, 0, THIN)
        local(keep, OWN)

        pair_copy().wait_recv()
        local(multiply, PAIR)
        multiply(PAIR, 1, 0, THIN)
        right_copy(1).wait_recv()

        @pl.loop(0, 2)
        def _(group):
            multiply(group, 1, THIN, THIN)

        local(keep, PAIR)

        @pl.loop(0, 2)
        def _(group):
            keep(group, 1, 0, THIN)
            keep(group, 1, THIN, THIN)

        for below in (True, False):
            @pl.when(col == (0 if below else 1))
            def _():
                for step in range(groups):
                    edge_copy(step, below, 0, row).wait_recv()

        for act in (multiply, keep):
            act(EDGE, 1, 0, THIN)
            act(EDGE, 1, THIN, THIN)
            local(act, EDGE)

        for n in (2, 3):
            right_copy(n).wait_recv()

            for act in (multiply, keep):
                @pl.loop(0, 3)
                def _(group, act=act, n=n):
                    act(group, 1, n * THIN, THIN)

        @pl.when(inner)
        def _():
            near_copy(0, row).wait_recv()
            for act in (multiply, keep):
                for n in range(4):
                    act(NEAR, 1, n * THIN, THIN)
                local(act, NEAR)

    @pl.when(idle)
    def _():
        right_copy(0).wait_send()
        right_copy(2).start()
        for step in range(groups):
            edge(lambda copy: copy.wait_send(), step)

        @pl.when(inner)
        def _():
            near_copy(1 - col, row - toward).start()

        right_copy(1).wait_send()
        right_copy(3).start()
        out_ref[...] = jnp.zeros_like(out_ref)

        for which in range(2):
            here = slice(which * THIN, (which + 1) * THIN)

            def arrived(index):
                relay = pltpu.make_async_remote_copy(
                    relay_out.at[:, :, here], relay_in.at[index, :, :, here],
                    relay_send.at[which], relay_recv.at[index, which],
                    device_id={"col": 1 - col}, device_id_type=MESH)
                relay.wait_recv()

            for near_half in range(2):
                @pl.when(1 - col == near_half)
                def _(near_half=near_half):
                    @pl.when(inner)
                    def _():
                        arrived(1 - near_half)
                        arrived(near_half)
                        relay_out[:, :, here] = (
                            relay_in[0, :, :, here].astype(jnp.float32) + relay_in[1, :, :, here].astype(jnp.float32)
                        ).astype(jnp.bfloat16)

                    @pl.when(jnp.logical_not(inner))
                    def _():
                        arrived(near_half)
                        relay_out[:, :, here] = relay_in[near_half, :, :, here]

            forward_copy(which).start()

    for source in (0, 3, 1, 2):
        far = jnp.abs(row - source)
        crosses = col != source // 2

        direct = (far <= 2) & jnp.logical_not(computes & (far == 0)) & jnp.logical_not(computes & crosses)
        relayed = computes & crosses & (source % 2 == 0)

        @pl.when(direct | relayed)
        def _():
            def arrive(which, lanes):
                pltpu.make_async_remote_copy(
                    send_out.at[0, 0, :, :, lanes], recv_out.at[source, :, :, lanes],
                    out_send.at[0, 0, 0], out_recv.at[source, which],
                    device_id={"ka": 1 - ka}, device_id_type=MESH).wait_recv()

            @pl.when(crosses)
            def _():
                arrive(0, pl.ds(0, THIN))
                arrive(1, pl.ds(THIN, THIN))

            @pl.when(jnp.logical_not(crosses))
            def _():
                arrive(0, pl.ds(0, wide))

            out_ref[...] += recv_out[source].astype(jnp.float32)

    @pl.when(computes)
    def _():
        pair_copy().wait_send()
        for group in range(4):
            def done(group=group):
                for sel, size in ((0, wide), (1, THIN)):
                    for start in range(0, 2 * wide, size):
                        @pl.when(ka != start // wide)
                        def _():
                            part_copy(group, sel, start, size).wait_send()

                        if (group, sel) != (OWN, 0):
                            @pl.when(ka == start // wide)
                            def _():
                                out_copy(group, sel, start, size).wait_send()

            if group == NEAR:
                pl.when(inner)(done)
            else:
                done()

    @pl.when(idle)
    def _():
        right_copy(2).wait_send()
        right_copy(3).wait_send()
        forward_copy(0).wait_send()
        forward_copy(1).wait_send()

        @pl.when(inner)
        def _():
            near_copy(1 - col, row - toward).wait_send()


def fused(left_data, right_data, taper_table, pattern, taper_index):
    _, rows, blocks, width = left_data.shape
    depth = right_data.shape[1] * width
    sources = right_data.shape[3]
    right = right_data.reshape(2, depth, sources)
    wide = sources // 2
    dma = pltpu.SemaphoreType.DMA
    vmem, whole = pl.BlockSpec(memory_space=pltpu.VMEM), pl.BlockSpec(memory_space=pl.ANY)
    return pl.pallas_call(
        kernel,
        out_shape=jax.ShapeDtypeStruct((2, rows, wide), jnp.float32),
        in_specs=[whole, whole, vmem, vmem, vmem],
        out_specs=vmem,
        scratch_shapes=[
            pltpu.VMEM(left_data.shape, jnp.bfloat16),
            pltpu.VMEM((2, 128, 128), jnp.float32),
            pltpu.VMEM((pattern.shape[0], blocks, width), jnp.float32),
            pltpu.VMEM((4, rows // pattern.shape[0] * blocks, width), jnp.float32),
            pltpu.VMEM((2, 2, rows, depth), jnp.bfloat16),
            pltpu.VMEM((4, 2, rows, depth), jnp.bfloat16),
            pltpu.VMEM((2, 2, depth, sources), jnp.bfloat16),
            pltpu.VMEM((4, 2, 2, rows, sources), jnp.float32),
            pltpu.VMEM((4, 2, 2, rows, wide), jnp.float32),
            pltpu.VMEM((4, 2, 2, rows, wide), jnp.bfloat16),
            pltpu.VMEM((4, 2, rows, wide), jnp.bfloat16),
            pltpu.VMEM((2, 2, rows, wide), jnp.bfloat16),
            pltpu.VMEM((2, rows, wide), jnp.bfloat16),
            dma((2,)), dma((2,)), dma((2,)), dma((8,)), dma((8,)), dma((4,)), dma((4,)),
            dma((4, 2, 2)), dma((4, 2, 2)), dma((4, 2, 2)), dma((4, 2)), dma((2, 2)), dma((2,)),
        ],
        compiler_params=pltpu.CompilerParams(
            collective_id=0, has_side_effects=True, vmem_limit_bytes=60 * 1024 * 1024
        ),
    )(left_data, right, taper_table, pattern, taper_index)


def fits(mesh, left_data, right_data, pattern):
    n_row, n_col, n_ka = mesh.shape["row"], mesh.shape["col"], mesh.shape["ka"]
    blocks = left_data.shape[2]
    return (
        n_row == 4 and n_col == 2 and n_ka == 2 and blocks == 32 and pattern.shape[0] == 2 * blocks
        and left_data.shape[1] == 1024 and left_data.shape[3] == 256 and right_data.shape[3] == 1024
    )


def solution(mesh):
    placed = (
        P("grp", "row", "col", "ka"),
        P("grp", "row", "ka", "col"),
        P(),
        P("row", None),
        P("row", None),
    )

    def run(left_data, right_data, taper_table, pattern, taper_index):
        step = fused if fits(mesh, left_data, right_data, pattern) else local
        return jax.shard_map(
            step, mesh=mesh, in_specs=placed, out_specs=P("grp", "row", ("col", "ka")), check_vma=False
        )(left_data, right_data, taper_table, pattern, taper_index)

    return run
```

```python
import jax
import jax.numpy as jnp
from jax import lax
from jax.experimental import pallas as pl
from jax.experimental.pallas import tpu as pltpu
from jax.sharding import PartitionSpec as P


def blend(left_data, taper_table, pattern, taper_index):
    col_part = left_data.shape[2]
    width = left_data.shape[3]
    rows = left_data.shape[1]
    blocks = pattern.shape[0]
    col_start = lax.axis_index("col") * col_part
    ka_start = lax.axis_index("ka") * width
    used = lax.dynamic_slice_in_dim(pattern, col_start, col_part, 1).astype(jnp.float32)
    levels = lax.dynamic_slice_in_dim(taper_index, col_start, col_part, 1)
    table = lax.dynamic_slice_in_dim(taper_table, ka_start, width, 1)
    onehot = (
        levels[:, :, None] == jnp.arange(taper_table.shape[0], dtype=jnp.int32)[None, None, :]
    ).astype(jnp.float32)
    weights = used[:, :, None] * jnp.einsum(
        "bjt,tw->bjw", onehot, table, precision=lax.Precision.HIGHEST
    )
    shaped = (
        left_data.astype(jnp.float32).reshape(2, blocks, rows // blocks, col_part, width)
        * weights[None, :, None]
    )
    return shaped.reshape(left_data.shape).astype(jnp.bfloat16)


def make_step(panel):

    def contract(piece):
        terms = jnp.einsum("crjw,djws->cdrs", panel, piece, preferred_element_type=jnp.float32)
        return jnp.stack([terms[0, 0] - terms[1, 1], terms[0, 1] + terms[1, 0]])

    def step(carry, piece, start):
        return contract(piece)

    return step


def local(left_data, right_data, taper_table, pattern, taper_index):
    weighted = blend(left_data, taper_table, pattern, taper_index)
    rows = left_data.shape[1]
    halves = lax.all_gather(weighted, "ka", axis=3, tiled=True)
    panel = lax.all_gather(halves, "col", axis=2, tiled=True)
    columns = lax.all_to_all(right_data, "ka", split_axis=3, concat_axis=2, tiled=True)
    start_sum = jnp.zeros((2, rows, columns.shape[3]), jnp.float32)
    result = make_step(panel)(
        start_sum, lax.all_gather(columns, "row", axis=1, tiled=True), jnp.int32(0)
    )
    return result


MESH = pl.DeviceIdType.MESH
BAND = 32
THIN = 128
OWN, PAIR, EDGE, NEAR = 0, 1, 2, 3


def weigh(raw, table_ref, pattern_ref, index_ref, turned, weights, loose, panel, col, ka, ready):
    blocks, points = raw.shape[2], raw.shape[3]
    depth = panel.shape[3]
    turned[...] = jnp.zeros_like(turned)
    levels, many = pattern_ref.shape
    turned[0, 0:levels, 0:many] = pattern_ref[...].astype(jnp.float32)
    turned[1, 0:levels, 0:many] = index_ref[...].astype(jnp.float32)
    used = turned[0].T
    level = turned[1].T
    turned[0] = used
    turned[1] = level
    mine = pl.ds(pl.multiple_of(col * blocks, blocks), blocks)
    table = table_ref[:, pl.ds(pl.multiple_of(ka * points, points), points)]
    for block in range(levels):
        column = turned[1, mine, block:block + 1]
        total = jnp.zeros((blocks, points), jnp.float32)
        for tap in range(table.shape[0]):
            total = jnp.where(column == tap, table[tap:tap + 1, :], total)
        weights[block] = total * turned[0, mine, block:block + 1]
    tall = raw.shape[1] // levels
    per = depth // points
    for block in range(levels):
        for part in range(2):
            slot = (2 * block + part) % loose.shape[0]
            rows = slice(block * tall, (block + 1) * tall)
            values = raw[part, rows].astype(jnp.float32) * weights[block][None]
            loose[slot] = values.reshape(tall * blocks, points)
            for j in range(blocks):
                lane = (j % per) * points
                panel[j // per, part, rows, lane:lane + points] = loose[
                    slot, pl.ds(j, tall, stride=blocks), :].astype(jnp.bfloat16)
        if (block + 1) * tall % BAND == 0:
            ready((block + 1) * tall // BAND - 1)


def kernel(left_ref, right_ref, table_ref, pattern_ref, index_ref, out_ref,
           raw, turned, weights, loose, panel, left, rights, part_out, given, part_in, send_out, recv_out,
           loc_sem, pair_sem, near_sem, edge_send, edge_recv, right_send, right_recv,
           part_send, part_recv, out_send, out_recv):
    row, col, ka = lax.axis_index("row"), lax.axis_index("col"), lax.axis_index("ka")
    side = row // 2
    half = row % 2
    computes = side == col
    idle = jnp.logical_not(computes)
    toward = 1 - 2 * col
    inner = (row == 1) | (row == 2)
    depth = left.shape[3]
    groups = depth // 128
    wide = out_ref.shape[2]

    own_raw = pltpu.make_async_copy(left_ref, raw, loc_sem.at[0])
    own_raw.start()
    left[EDGE] = jnp.zeros(left.shape[1:], left.dtype)

    barrier = pltpu.get_barrier_semaphore()
    for step in range(1, 8):
        to = (row * 2 + col + step) % 8
        pl.semaphore_signal(barrier, inc=1, device_id={"row": to // 2, "col": to % 2}, device_id_type=MESH)
    pl.semaphore_signal(barrier, inc=1, device_id={"ka": 1 - ka}, device_id_type=MESH)
    pl.semaphore_wait(barrier, 8)

    def pair_copy():
        return pltpu.make_async_remote_copy(
            panel.at[1 - half], left.at[PAIR], pair_sem.at[0], pair_sem.at[1],
            device_id={"row": 2 * side + 1 - half}, device_id_type=MESH)

    def near_copy(src_half, to_row):
        return pltpu.make_async_remote_copy(
            panel.at[src_half], left.at[NEAR], near_sem.at[0], near_sem.at[1],
            device_id={"row": to_row}, device_id_type=MESH)

    def edge_copy(step, below, src_half, to_row):
        band = pl.ds(BAND * step, BAND)
        lanes = pl.ds(128 * step, depth - 128 * step) if below else pl.ds(0, 128 * (step + 1))
        return pltpu.make_async_remote_copy(
            panel.at[src_half, :, band, lanes], left.at[EDGE, :, band, lanes],
            edge_send.at[step], edge_recv.at[step],
            device_id={"row": to_row}, device_id_type=MESH)

    def edge(act, step):
        to_row = row - 2 * toward
        for below in (True, False):
            @pl.when(idle & (col == (0 if below else 1)))
            def _():
                act(edge_copy(step, below, to_row % 2, to_row))

    def right_copy(n):
        lanes = pl.ds(THIN * n, THIN)
        return pltpu.make_async_remote_copy(
            right_ref.at[:, :, lanes], rights.at[1, :, :, lanes],
            right_send.at[n], right_recv.at[n],
            device_id={"col": 1 - col}, device_id_type=MESH)

    def own_left():
        return pltpu.make_async_copy(panel.at[half], left.at[OWN], loc_sem.at[0])

    def own_right():
        return pltpu.make_async_copy(right_ref, rights.at[0], loc_sem.at[1])

    @pl.when(idle)
    def _():
        right_copy(0).start()
        right_copy(1).start()

    pl.when(computes)(lambda: own_right().start())

    own_raw.wait()
    weigh(raw, table_ref, pattern_ref, index_ref, turned, weights, loose, panel, col, ka,
          lambda step: edge(lambda copy: copy.start(), step))

    def part_copy(group, sel, start, size):
        here = pl.ds(start % wide, size)
        return pltpu.make_async_remote_copy(
            given.at[group, sel, :, :, pl.ds(start, size)], part_in.at[group, sel, :, :, here],
            part_send.at[group, sel, start // size % 2 if sel else 0],
            part_recv.at[group, sel, start // size % 2 if sel else 0],
            device_id={"ka": 1 - ka}, device_id_type=MESH)

    def row_of(group):
        pair = row + 1 - 2 * half
        return jnp.where(group == OWN, row, jnp.where(group == PAIR, pair, jnp.where(
            group == EDGE, row + 2 * toward, row + toward)))

    def out_copy(group, sel, start, size):
        here = pl.ds(start % wide, size)
        to_col = col if sel == 0 else 1 - col
        which = start // size % 2 if sel else 0
        return pltpu.make_async_remote_copy(
            send_out.at[group, sel, :, :, here], recv_out.at[row, :, :, here],
            out_send.at[group, sel, which], out_recv.at[row, which],
            device_id={"row": row_of(group), "col": to_col}, device_id_type=MESH)

    def multiply(group, sel, start, size):
        lanes = slice(start, start + size)
        dot = lambda a, b: jnp.dot(left[group, a], rights[sel, b, :, lanes], preferred_element_type=jnp.float32)
        part_out[group, sel, 0, :, lanes] = dot(0, 0) - dot(1, 1)
        part_out[group, sel, 1, :, lanes] = dot(0, 1) + dot(1, 0)

        @pl.when(ka != start // wide)
        def _():
            given[group, sel, :, :, lanes] = part_out[group, sel, :, :, lanes].astype(jnp.bfloat16)
            part_copy(group, sel, start, size).start()

    def keep(group, sel, start, size):
        lanes = slice(start, start + size)
        here = slice(start % wide, start % wide + size)

        @pl.when(ka == start // wide)
        def _():
            part_copy(group, sel, start, size).wait_recv()

            def total():
                return part_out[group, sel, :, :, lanes] + part_in[group, sel, :, :, here].astype(jnp.float32)

            def send():
                send_out[group, sel, :, :, here] = total().astype(jnp.bfloat16)
                out_copy(group, sel, start, size).start()

            if sel == 1:
                send()
            else:
                @pl.when(group == OWN)
                def _():
                    out_ref[...] = total()

                pl.when(group != OWN)(send)

    def local(act, group):
        for start in range(0, 2 * wide, wide):
            act(group, 0, start, wide)

    @pl.when(computes)
    def _():
        pair_copy().start()
        own_left().start()
        own_right().wait()
        own_left().wait()

        local(multiply, OWN)
        right_copy(0).wait_recv()
        multiply(OWN, 1, 0, THIN)
        local(keep, OWN)

        pair_copy().wait_recv()
        local(multiply, PAIR)
        multiply(PAIR, 1, 0, THIN)
        right_copy(1).wait_recv()

        @pl.loop(0, 2)
        def _(group):
            multiply(group, 1, THIN, THIN)

        local(keep, PAIR)

        @pl.loop(0, 2)
        def _(group):
            keep(group, 1, 0, THIN)
            keep(group, 1, THIN, THIN)

        for below in (True, False):
            @pl.when(col == (0 if below else 1))
            def _():
                for step in range(groups):
                    edge_copy(step, below, 0, row).wait_recv()

        for act in (multiply, keep):
            act(EDGE, 1, 0, THIN)
            act(EDGE, 1, THIN, THIN)
            local(act, EDGE)

        for n in (2, 3):
            right_copy(n).wait_recv()

            for act in (multiply, keep):
                @pl.loop(0, 3)
                def _(group, act=act, n=n):
                    act(group, 1, n * THIN, THIN)

        @pl.when(inner)
        def _():
            near_copy(0, row).wait_recv()
            for act in (multiply, keep):
                for n in range(4):
                    act(NEAR, 1, n * THIN, THIN)
                local(act, NEAR)

    @pl.when(idle)
    def _():
        right_copy(0).wait_send()
        right_copy(2).start()
        for step in range(groups):
            edge(lambda copy: copy.wait_send(), step)

        @pl.when(inner)
        def _():
            near_copy(1 - col, row - toward).start()

        right_copy(1).wait_send()
        right_copy(3).start()
        out_ref[...] = jnp.zeros_like(out_ref)

    for source in (0, 3, 1, 2):
        far = jnp.abs(row - source)
        crosses = col != source // 2

        @pl.when((far <= 2) & jnp.logical_not(computes & (far == 0)))
        def _():
            def arrive(which, lanes):
                pltpu.make_async_remote_copy(
                    send_out.at[0, 0, :, :, lanes], recv_out.at[source, :, :, lanes],
                    out_send.at[0, 0, 0], out_recv.at[source, which],
                    device_id={"ka": 1 - ka}, device_id_type=MESH).wait_recv()

            @pl.when(crosses)
            def _():
                arrive(0, pl.ds(0, THIN))
                arrive(1, pl.ds(THIN, THIN))

            @pl.when(jnp.logical_not(crosses))
            def _():
                arrive(0, pl.ds(0, wide))

            out_ref[...] += recv_out[source].astype(jnp.float32)

    @pl.when(computes)
    def _():
        pair_copy().wait_send()
        for group in range(4):
            def done(group=group):
                for sel, size in ((0, wide), (1, THIN)):
                    for start in range(0, 2 * wide, size):
                        @pl.when(ka != start // wide)
                        def _():
                            part_copy(group, sel, start, size).wait_send()

                        if (group, sel) != (OWN, 0):
                            @pl.when(ka == start // wide)
                            def _():
                                out_copy(group, sel, start, size).wait_send()

            if group == NEAR:
                pl.when(inner)(done)
            else:
                done()

    @pl.when(idle)
    def _():
        right_copy(2).wait_send()
        right_copy(3).wait_send()

        @pl.when(inner)
        def _():
            near_copy(1 - col, row - toward).wait_send()


def fused(left_data, right_data, taper_table, pattern, taper_index):
    _, rows, blocks, width = left_data.shape
    depth = right_data.shape[1] * width
    sources = right_data.shape[3]
    right = right_data.reshape(2, depth, sources)
    wide = sources // 2
    dma = pltpu.SemaphoreType.DMA
    vmem, whole = pl.BlockSpec(memory_space=pltpu.VMEM), pl.BlockSpec(memory_space=pl.ANY)
    return pl.pallas_call(
        kernel,
        out_shape=jax.ShapeDtypeStruct((2, rows, wide), jnp.float32),
        in_specs=[whole, whole, vmem, vmem, vmem],
        out_specs=vmem,
        scratch_shapes=[
            pltpu.VMEM(left_data.shape, jnp.bfloat16),
            pltpu.VMEM((2, 128, 128), jnp.float32),
            pltpu.VMEM((pattern.shape[0], blocks, width), jnp.float32),
            pltpu.VMEM((4, rows // pattern.shape[0] * blocks, width), jnp.float32),
            pltpu.VMEM((2, 2, rows, depth), jnp.bfloat16),
            pltpu.VMEM((4, 2, rows, depth), jnp.bfloat16),
            pltpu.VMEM((2, 2, depth, sources), jnp.bfloat16),
            pltpu.VMEM((4, 2, 2, rows, sources), jnp.float32),
            pltpu.VMEM((4, 2, 2, rows, sources), jnp.bfloat16),
            pltpu.VMEM((4, 2, 2, rows, wide), jnp.bfloat16),
            pltpu.VMEM((4, 2, 2, rows, wide), jnp.bfloat16),
            pltpu.VMEM((4, 2, rows, wide), jnp.bfloat16),
            dma((2,)), dma((2,)), dma((2,)), dma((8,)), dma((8,)), dma((4,)), dma((4,)),
            dma((4, 2, 2)), dma((4, 2, 2)), dma((4, 2, 2)), dma((4, 2)),
        ],
        compiler_params=pltpu.CompilerParams(
            collective_id=0, has_side_effects=True, vmem_limit_bytes=60 * 1024 * 1024
        ),
    )(left_data, right, taper_table, pattern, taper_index)


def fits(mesh, left_data, right_data, pattern):
    n_row, n_col, n_ka = mesh.shape["row"], mesh.shape["col"], mesh.shape["ka"]
    blocks = left_data.shape[2]
    return (
        n_row == 4 and n_col == 2 and n_ka == 2 and blocks == 32 and pattern.shape[0] == 2 * blocks
        and left_data.shape[1] == 1024 and left_data.shape[3] == 256 and right_data.shape[3] == 1024
    )


def solution(mesh):
    placed = (
        P("grp", "row", "col", "ka"),
        P("grp", "row", "ka", "col"),
        P(),
        P("row", None),
        P("row", None),
    )

    def run(left_data, right_data, taper_table, pattern, taper_index):
        step = fused if fits(mesh, left_data, right_data, pattern) else local
        return jax.shard_map(
            step, mesh=mesh, in_specs=placed, out_specs=P("grp", "row", ("col", "ka")), check_vma=False
        )(left_data, right_data, taper_table, pattern, taper_index)

    return run
```
